32 devices in a mesh: dp: 4 (over y, core), px: 2 (over x), py: 4 (over z).
Axes of the slice: x: 2, y: 2, z: 4, core: 2. Of those that a mesh axis runs over, the one named last changes fastest.
Arguments:
- state_field: bfloat16 [4, 64, 64, 32, 384], P('dp', 'px', 'py'), may hold values from -6 to 6
- cotangent: bfloat16 [4, 64, 64, 32, 384], P('dp', 'px', 'py'), may hold values from -6 to 6
- first_weight: float32 [2, 4, 96, 96], replicated, may hold values from -0.4375 to 0.4375
- first_bias: float32 [2, 4, 96], replicated, may hold values from -3 to 3
- second_weight: float32 [2, 4, 96, 96], replicated, may hold values from -0.4375 to 0.4375
- second_bias: float32 [2, 4, 96], replicated, may hold values from -3 to 3
Outputs:
- state_grad: bfloat16 [4, 64, 64, 32, 384], P('dp', 'px', 'py')
- first_weight_grad: float32 [2, 4, 96, 96], replicated
- first_bias_grad: float32 [2, 4, 96], replicated
- second_weight_grad: float32 [2, 4, 96, 96], replicated
- second_bias_grad: float32 [2, 4, 96], replicated
The draws below stay inside these ranges and needn't reach their ends.
All inputs are finite; a program needn't handle non-finite values.
Results may differ from the reference program's by a relative error of at most 0.001.
Values sent between devices are 32-bit elements; how exact they have to be, the bound alone decides.
A program may use at most 320 MiB of HBM per device.

```python
import math
import jax
import jax.numpy as jnp
from jax import lax

NX = 64
NY = 64
NZ = 32
NB = 4
BS = 96
KZ = 16
C = 384
SAMPLES = 4


def steps_of(stream_key, shape, split, least, largest):
    def one(dim, blocks):
        heights = jax.random.uniform(jax.random.fold_in(jax.random.fold_in(stream_key, 6), dim), (blocks,), jnp.float32, least / len(split), largest / len(split))
        return jnp.repeat(jnp.exp(heights), shape[dim] // blocks).reshape((-1,) + (1,) * (len(shape) - dim - 1))

    gain = one(*split[0])
    for cut in split[1:]:
        gain = gain * one(*cut)
    return gain


def noise(key, shape, deviation, reach, pieces=(), held_as=jnp.bfloat16):
    gain = steps_of(key, shape, pieces, -0.22, 0.18) if pieces else 1.0
    entries = jax.random.normal(key, shape, jnp.float32) * deviation * gain
    return jnp.minimum(jnp.maximum(entries, -reach), reach).astype(held_as)


def setup_inputs(seed: int = 0) -> dict:
    seeds = jax.random.split(jax.random.key(seed), 7)
    state_field = noise(seeds[0], (SAMPLES, NX, NY, NZ, C), 1.0, 6.0, ((0, 4), (1, 2), (2, 4)))
    cotangent = noise(seeds[1], (SAMPLES, NX, NY, NZ, C), 1.0, 6.0, ((0, 4), (1, 2), (2, 4)))
    first_weight = noise(seeds[2], (2, NB, BS, BS), (2 * BS) ** -0.5, 0.4375, (), jnp.float32)
    first_bias = noise(seeds[3], (2, NB, BS), 0.5, 3.0, (), jnp.float32)
    second_weight = noise(seeds[4], (2, NB, BS, BS), (2 * BS) ** -0.5, 0.4375, (), jnp.float32)
    second_bias = noise(seeds[5], (2, NB, BS), 0.5, 3.0, (), jnp.float32)
    return {"state_field": state_field, "cotangent": cotangent, "first_weight": first_weight, "first_bias": first_bias, "second_weight": second_weight, "second_bias": second_bias}


shrink_level = 0.25
highest = lax.Precision.HIGHEST

def pair_table(weight):
    real_part = weight[0]
    imag_part = weight[1]
    upper_half = jnp.stack([real_part, imag_part], axis=2)
    lower_half = jnp.stack([-imag_part, real_part], axis=2)
    return jnp.stack([upper_half, lower_half], axis=0)

def fold_pairs(pair_grads):
    return jnp.stack([pair_grads[0, :, :, 0] + pair_grads[1, :, :, 1], pair_grads[0, :, :, 1] - pair_grads[1, :, :, 0]])

def contract(pattern, left_side, right_side):
    return jnp.einsum(pattern, left_side, right_side, precision=highest, preferred_element_type=jnp.float32)

def spectrum_of(field_values):
    full_spectrum = jnp.fft.rfftn(field_values, axes=(0, 1, 2), norm='ortho')[:, :, :KZ, :]
    return jnp.stack([jnp.real(full_spectrum), jnp.imag(full_spectrum)])

def field_of(spectral):
    kz_ids = jnp.arange(KZ, dtype=jnp.int32)
    halving = jnp.where(kz_ids == 0, 1.0, 0.5).astype(spectral.dtype)[:, None]
    values = lax.complex(spectral[0] * halving, spectral[1] * halving)
    padding = jnp.zeros((NX, NY, NZ // 2 + 1 - KZ, NB * BS), values.dtype)
    padded = jnp.concatenate([values, padding], axis=2)
    return jnp.fft.irfftn(padded, s=(NX, NY, NZ), axes=(0, 1, 2), norm='ortho')

def reference(state_field, cotangent, first_weight, first_bias, second_weight, second_bias):
    first_table = pair_table(first_weight)
    second_table = pair_table(second_weight)
    kz_ids = jnp.arange(KZ, dtype=jnp.int32)
    doubling = jnp.where(kz_ids == 0, 1.0, 2.0).astype(jnp.float32)[:, None]

    def one_sample(totals, inputs):
        sample_field, sample_cotangent = inputs
        spectral_full = spectrum_of(sample_field.astype(jnp.float32))
        shape_full = spectral_full.shape
        spectral_in = spectral_full.reshape(2, -1, NB, BS)
        gradient_in = (spectrum_of(sample_cotangent.astype(jnp.float32)) * doubling).reshape(2, -1, NB, BS)
        pre_one = contract('rfbi,rbiqo->qfbo', spectral_in, first_table) + first_bias[:, None]
        outer_one, gelu_back = jax.vjp(jax.nn.gelu, pre_one)
        pre_two = contract('rfbi,rbiqo->qfbo', outer_one, second_table) + second_bias[:, None]
        grad_two = gradient_in * jnp.tanh(pre_two / shrink_level) ** 2
        table_two = contract('rfbi,qfbo->rbiqo', outer_one, grad_two)
        grad_outer = contract('qfbo,rbiqo->rfbi', grad_two, second_table)
        grad_one = gelu_back(grad_outer)[0]
        table_one = contract('rfbi,qfbo->rbiqo', spectral_in, grad_one)
        grad_spec = contract('qfbo,rbiqo->rfbi', grad_one, first_table)
        spatial = field_of(grad_spec.reshape(shape_full))
        state_grad = (sample_cotangent.astype(jnp.float32) + spatial).astype(jnp.bfloat16)
        totals = (totals[0] + fold_pairs(table_one), totals[1] + lax.optimization_barrier(jnp.sum(grad_one, axis=1)), totals[2] + fold_pairs(table_two), totals[3] + lax.optimization_barrier(jnp.sum(grad_two, axis=1)))
        return (totals, state_grad)
    zeros_weight = jnp.zeros((2, NB, BS, BS), jnp.float32)
    zeros_bias = jnp.zeros((2, NB, BS), jnp.float32)
    totals, state_grad = lax.scan(one_sample, (zeros_weight, zeros_bias, zeros_weight, zeros_bias), (state_field, cotangent))
    norm_factor = 1.0 / math.sqrt(SAMPLES * NX * NY * KZ)
    return (state_grad, totals[0] * norm_factor, totals[1] * norm_factor, totals[2] * norm_factor, totals[3] * norm_factor)
```

```python
import math

import jax
import jax.numpy as jnp
from jax import lax
from jax.experimental import pallas as pl
from jax.experimental.pallas import tpu as pltpu
from jax.sharding import PartitionSpec as P

NX = 64
NY = 64
NZ = 32
NB = 4
BS = 96
KZ = 16


shrink_level = 0.25
highest = lax.Precision.HIGHEST


def complex_table(length, modes):
    row_ids = jnp.arange(length, dtype=jnp.int32)[:, None]
    col_ids = jnp.arange(modes, dtype=jnp.int32)[None, :]
    angles = (row_ids * col_ids % length).astype(jnp.float32) * (2.0 * math.pi / length)
    factor = 1.0 / math.sqrt(length)
    cosine = jnp.cos(angles) * factor
    sine_part = jnp.sin(angles) * factor
    upper_half = jnp.stack([cosine, -sine_part], axis=1)
    lower_half = jnp.stack([sine_part, cosine], axis=1)
    return jnp.stack([upper_half, lower_half], axis=0)


def pair_table(weight):
    real_part = weight[0]
    imag_part = weight[1]
    upper_half = jnp.stack([real_part, imag_part], axis=2)
    lower_half = jnp.stack([-imag_part, real_part], axis=2)
    return jnp.stack([upper_half, lower_half], axis=0)


def fold_pairs(pair_grads):
    return jnp.stack(
        [
            pair_grads[0, :, :, 0] + pair_grads[1, :, :, 1],
            pair_grads[0, :, :, 1] - pair_grads[1, :, :, 0],
        ]
    )


def contract(pattern, left_side, right_side):
    return jnp.einsum(
        pattern, left_side, right_side, precision=highest, preferred_element_type=jnp.float32
    )


def along_rows(spectral, rows_table):
    return contract("rmsxyzc,rxqk->qmskyzc", spectral, rows_table)


def along_cols(spectral, cols_table):
    return contract("rmsxyzc,ryqk->qmsxkzc", spectral, cols_table)


def back_rows(spectral, rows_table):
    return contract("qmskyzc,rxqk->rmsxyzc", spectral, rows_table)


def back_cols(spectral, cols_table):
    return contract("qmsxkzc,ryqk->rmsxyzc", spectral, cols_table)


def back_depth(spectral, depth_table):
    return contract("qmsxykc,zqk->msxyzc", spectral, depth_table)


def to_spectrum(fields, depth_table, rows_table, cols_table):
    spectral = contract("msxyzc,zqk->qmsxykc", fields, depth_table)
    spectral = along_cols(
        lax.all_to_all(spectral, "py", split_axis=5, concat_axis=4, tiled=True),
        cols_table=cols_table,
    )
    spectral = along_rows(
        lax.all_to_all(spectral, "px", split_axis=4, concat_axis=3, tiled=True),
        rows_table=rows_table,
    )
    return spectral


def to_field(spectral, depth_table, rows_table, cols_table):
    spectral = back_rows(spectral, rows_table)
    spectral = back_cols(
        lax.all_to_all(spectral, "px", split_axis=3, concat_axis=4, tiled=True),
        cols_table=cols_table,
    )
    result = back_depth(
        lax.all_to_all(spectral, "py", split_axis=4, concat_axis=5, tiled=True),
        depth_table=depth_table,
    )
    return result


def mix_forward(flat_in, first_table, first_bias, second_table, second_bias):
    pre_one = contract("rfbi,rbiqo->qfbo", flat_in, first_table) + first_bias[:, None]
    outer_one, gelu_back = jax.vjp(jax.nn.gelu, pre_one)
    pre_two = contract("rfbi,rbiqo->qfbo", outer_one, second_table) + second_bias[:, None]
    return (outer_one, gelu_back, pre_two)


def shards_plain(state_field, cotangent, first_weight, first_bias, second_weight, second_bias):
    depth_table = complex_table(NZ, KZ)[0]
    rows_table = complex_table(NX, NX)
    cols_table = complex_table(NY, NY)
    full_first = pair_table(first_weight)
    full_second = pair_table(second_weight)
    group_count = NB
    kz_block = lax.axis_index("py")
    kz_local = KZ // lax.axis_size("py")
    kz_global = kz_block * kz_local + jnp.arange(kz_local, dtype=jnp.int32)
    spectral_in = to_spectrum(state_field[None], depth_table, rows_table, cols_table)
    flat_in = spectral_in.reshape(2, -1, group_count, BS)
    outer_one, gelu_back, pre_two = mix_forward(
        flat_in, full_first, first_bias, full_second, second_bias
    )
    raw_gradient = to_spectrum(cotangent[None], depth_table, rows_table, cols_table)
    shape_full = spectral_in.shape
    doubling = jnp.where(kz_global == 0, 1.0, 2.0).astype(jnp.float32)[:, None]
    gradient_in = (raw_gradient * doubling).reshape(2, -1, group_count, BS)
    grad_two = gradient_in * jnp.tanh(pre_two / shrink_level) ** 2
    table_two = contract("rfbi,qfbo->rbiqo", outer_one, grad_two)
    grad_outer = contract("qfbo,rbiqo->rfbi", grad_two, full_second)
    grad_one = gelu_back(grad_outer)[0]
    table_one = contract("rfbi,qfbo->rbiqo", flat_in, grad_one)
    grad_spec = contract("qfbo,rbiqo->rfbi", grad_one, full_first)
    bias_one = jnp.sum(grad_one, axis=1)
    bias_two = jnp.sum(grad_two, axis=1)
    total_freq = state_field.shape[0] * lax.axis_size("dp") * NX * NY * KZ
    norm_factor = 1.0 / math.sqrt(total_freq)
    sums = lax.psum(
        (
            fold_pairs(table_one) * norm_factor,
            bias_one * norm_factor,
            fold_pairs(table_two) * norm_factor,
            bias_two * norm_factor,
        ),
        ("dp", "px", "py"),
    )
    spatial = to_field(grad_spec.reshape(shape_full), depth_table, rows_table, cols_table)[0]
    state_grad = (cotangent.astype(jnp.float32) + spatial).astype(jnp.bfloat16)
    return (state_grad, sums[0], sums[1], sums[2], sums[3])


C = NB * BS
LANES = 128
GROUPS = C // LANES
CELL_BLOCK = 64
KY_BLOCK = 8
VMEM = 60 * 1024 * 1024
f32 = jnp.float32
bf16 = jnp.bfloat16


def first_group(block):
    return block * BS // LANES


def group_count_of(block):
    return ((block + 1) * BS - 1) // LANES - first_group(block) + 1


WINDOWS = [(first_group(b), group_count_of(b)) for b in range(NB)]


def halves(values):
    high = lax.reduce_precision(values, 8, 7)
    return high.astype(bf16), (values - high).astype(bf16)


def split(values):
    high = values.astype(bf16)
    return high, (values - high.astype(f32)).astype(bf16)


def dot(left, right, dims=(((1,), (0,)), ((), ()))):
    return lax.dot_general(left, right, dims, preferred_element_type=f32)


def dot3(left, right, dims=(((1,), (0,)), ((), ()))):
    return (
        dot(left[0], right[0], dims) + dot(left[1], right[0], dims) + dot(left[0], right[1], dims)
    )


def table_dot(wide, low, values):
    high, rest = split(values)
    return dot(wide, jnp.concatenate([high, rest], axis=0)) + dot(low, high)


def angle_tables(length, rows, cols):
    angles = (rows[:, None] * cols[None, :] % length).astype(f32) * (2.0 * math.pi / length)
    factor = 1.0 / math.sqrt(length)
    return jnp.cos(angles) * factor, jnp.sin(angles) * factor


def table_pair(table):
    high, low = halves(table)
    return jnp.concatenate([high, high], axis=1), low


def depth_forward(field, table, slots, cells):
    def body(high_ref, low_ref, field_ref, *outs):
        for step in range(CELL_BLOCK // 8):
            part = field_ref[pl.ds(step * 8 * NZ, 8 * NZ), :]
            result = dot(high_ref[...], part) + dot(low_ref[...], part)
            for place, out in enumerate(outs):
                for r in range(2):
                    row = (place * 2 + r) * 8
                    out[r, pl.ds(step * 8, 8), :] = result[row : row + 8]

    size = 8 * NZ
    whole = pl.BlockSpec((size, size), lambda i: (0, 0))
    return pl.pallas_call(
        body,
        grid=(cells // CELL_BLOCK,),
        in_specs=[whole, whole, pl.BlockSpec((CELL_BLOCK * NZ, C), lambda i: (i, 0))],
        out_specs=[pl.BlockSpec((2, CELL_BLOCK, C), lambda i: (0, i, 0))] * slots,
        out_shape=[jax.ShapeDtypeStruct((2, cells, C), f32)] * slots,
        compiler_params=pltpu.CompilerParams(vmem_limit_bytes=VMEM),
        cost_estimate=pl.CostEstimate(
            flops=cells * 32 * C * size * 4, bytes_accessed=cells * 32 * C * 6, transcendentals=0
        ),
        name="depth_forward",
    )(*halves(table), field)


def depth_back(parts, cotangent, table, cells):
    slots = len(parts)

    def body(wide_ref, low_ref, cot_ref, *refs):
        out = refs[-1]
        for step in range(CELL_BLOCK // 8):
            rows = pl.ds(step * 8, 8)
            stacked = jnp.concatenate(
                [refs[place][r, rows, :] for place in range(slots) for r in range(2)], axis=0
            )
            here = pl.ds(step * 8 * NZ, 8 * NZ)
            spatial = table_dot(wide_ref[...], low_ref[...], stacked)
            out[here, :] = (cot_ref[here, :].astype(f32) + spatial).astype(bf16)

    size = 8 * NZ
    block = pl.BlockSpec((CELL_BLOCK * NZ, C), lambda i: (i, 0))
    return pl.pallas_call(
        body,
        grid=(cells // CELL_BLOCK,),
        in_specs=[
            pl.BlockSpec((size, 2 * size), lambda i: (0, 0)),
            pl.BlockSpec((size, size), lambda i: (0, 0)),
            block,
        ]
        + [pl.BlockSpec((2, CELL_BLOCK, C), lambda i: (0, i, 0))] * slots,
        out_specs=block,
        out_shape=jax.ShapeDtypeStruct((cells * NZ, C), bf16),
        compiler_params=pltpu.CompilerParams(vmem_limit_bytes=VMEM),
        cost_estimate=pl.CostEstimate(
            flops=cells * 32 * C * size * 6, bytes_accessed=cells * 32 * C * 8, transcendentals=0
        ),
        name="depth_back",
    )(*table_pair(table), cotangent, *parts)


def plane_call(body, operands, in_shapes, out_shapes, rows, name):
    vmem = pl.BlockSpec(memory_space=pltpu.VMEM)
    return pl.pallas_call(
        body,
        in_specs=[vmem] * len(operands),
        out_specs=[vmem] * len(out_shapes),
        out_shape=out_shapes,
        scratch_shapes=[pltpu.VMEM((GROUPS, rows, LANES), f32)],
        compiler_params=pltpu.CompilerParams(vmem_limit_bytes=VMEM),
        cost_estimate=pl.CostEstimate(
            flops=2 * 2 * NX * NY * C * 256 * 2 * 3,
            bytes_accessed=2 * NX * NY * C * 8,
            transcendentals=0,
        ),
        name=name,
    )(*operands)


def lanes_of(group):
    return slice(group * LANES, (group + 1) * LANES)


def plane_forward(parts, cols_table, rows_table, nx, ny):
    xl, yl = NX // nx, NY // ny
    pitch = NY + 8

    def body(cw, cl, rw, rl, *refs):
        ins, out, mid = refs[: nx * ny], refs[nx * ny], refs[nx * ny + 1]
        for dx in range(nx):

            def columns(i, carry, dx=dx):
                here = pl.ds(pl.multiple_of(i * yl, yl), yl)
                stacked = jnp.concatenate(
                    [ins[dx * ny + dy][r, here, :] for r in range(2) for dy in range(ny)], axis=0
                )
                result = table_dot(cw[...], cl[...], stacked)
                for r in range(2):
                    start = pl.multiple_of(((dx * xl + i) * 2 + r) * pitch, 8)
                    for g in range(GROUPS):
                        mid[g, pl.ds(start, NY), :] = result[r * NY : (r + 1) * NY, lanes_of(g)]
                return carry

            lax.fori_loop(0, xl, columns, 0, unroll=4)

        def across(ky, carry):
            stacked = jnp.concatenate(
                [mid[g, pl.ds(ky, 2 * NX, stride=pitch), :] for g in range(GROUPS)], axis=1
            )
            out[ky] = table_dot(rw[...], rl[...], stacked).reshape(2, NX, C)
            return carry

        lax.fori_loop(0, NY, across, 0, unroll=4)

    return plane_call(
        body,
        (*table_pair(cols_table), *table_pair(rows_table), *parts),
        None,
        [jax.ShapeDtypeStruct((NY, 2, NX, C), f32)],
        2 * NX * pitch,
        "plane_forward",
    )[0]


def plane_back(spectrum, cols_table, rows_table, nx, ny):
    xl, yl = NX // nx, NY // ny
    pitch = 2 * NX + 8

    def body(cw, cl, rw, rl, spec, *refs):
        outs, mid = refs[: nx * ny], refs[nx * ny]

        def across(ky, carry):
            result = table_dot(rw[...], rl[...], spec[ky].reshape(2 * NX, C))
            start = pl.multiple_of(ky * pitch, 8)
            for g in range(GROUPS):
                mid[g, pl.ds(start, 2 * NX), :] = result[:, lanes_of(g)]
            return carry

        lax.fori_loop(0, NY, across, 0, unroll=4)
        for dx in range(nx):

            def columns(i, carry, dx=dx):
                stacked = jnp.concatenate(
                    [
                        jnp.concatenate(
                            [
                                mid[g, pl.ds((dx * xl + i) * 2 + r, NY, stride=pitch), :]
                                for g in range(GROUPS)
                            ],
                            axis=1,
                        )
                        for r in range(2)
                    ],
                    axis=0,
                )
                result = table_dot(cw[...], cl[...], stacked)
                here = pl.ds(pl.multiple_of(i * yl, yl), yl)
                for r in range(2):
                    for dy in range(ny):
                        row = (r * ny + dy) * yl
                        outs[dx * ny + dy][r, here, :] = result[row : row + yl]
                return carry

            lax.fori_loop(0, xl, columns, 0, unroll=4)

    return plane_call(
        body,
        (*table_pair(cols_table), *table_pair(rows_table), spectrum),
        None,
        [jax.ShapeDtypeStruct((2, xl * yl, C), f32)] * (nx * ny),
        NY * pitch,
        "plane_back",
    )


def window(pair, block):
    start, count = WINDOWS[block]
    lanes = slice(start * LANES, (start + count) * LANES)
    return jnp.concatenate([pair[0][:, lanes], pair[1][:, lanes]], axis=1)


def spread(results):
    sides = []
    for r in range(2):
        groups = [None] * GROUPS
        for block, result in enumerate(results):
            start, count = WINDOWS[block]
            for g in range(count):
                at = r * count + g
                part = result[:, at * LANES : (at + 1) * LANES]
                groups[start + g] = part if groups[start + g] is None else groups[start + g] + part
        sides.append(jnp.concatenate(groups, axis=1))
    return sides


def offset_of(block):
    return block * BS - WINDOWS[block][0] * LANES


def stack_windows(table, axes):
    pieces = []
    for block in range(NB):
        count = WINDOWS[block][1]
        before = offset_of(block)
        wide = (before, count * LANES - before - BS)
        slim = (0, LANES - BS)
        sides = (wide, slim) if axes == 0 else (slim, wide)
        piece = jnp.pad(table[:, block], ((0, 0), sides[0], (0, 0), sides[1]))
        piece = piece.reshape(2 * piece.shape[1], -1)
        pieces.append(piece)
    return jnp.concatenate(pieces, axis=axes)


def unstack_windows(stacked, axes):
    pieces = []
    at = 0
    for block in range(NB):
        count = WINDOWS[block][1]
        size = 2 * count * LANES
        before = offset_of(block)
        if axes == 0:
            piece = stacked[at : at + size].reshape(2, count * LANES, 2, LANES)
            piece = piece[:, before : before + BS, :, :BS]
        else:
            piece = stacked[:, at : at + size].reshape(2, LANES, 2, count * LANES)
            piece = piece[:, :BS, :, before : before + BS]
        pieces.append(piece)
        at += size
    return jnp.stack(pieces, axis=1)


OFFSETS = [sum(2 * w[1] * LANES for w in WINDOWS[:b]) for b in range(NB + 1)]
WIDE = OFFSETS[NB]
SLIM = 2 * LANES


def block_span(block):
    return slice(OFFSETS[block], OFFSETS[block + 1])


def slim_span(block):
    return slice(block * SLIM, (block + 1) * SLIM)


def plane_block():
    return pl.BlockSpec((KY_BLOCK, 2, NX, C), lambda i: (i, 0, 0, 0))


def whole_block(*shape):
    return pl.BlockSpec(shape, lambda i: (0,) * len(shape))


def mix_cost(count, reads):
    rows = NX * NY
    return pl.CostEstimate(
        flops=rows * WIDE * SLIM * 2 * 3 * count,
        bytes_accessed=rows * 2 * C * 4 * reads,
        transcendentals=rows * 2 * C * 2,
    )


def both_sides(ref):
    rows = KY_BLOCK * NX
    return ref[:, 0].reshape(rows, C), ref[:, 1].reshape(rows, C)


def mix_front(spectrum, first, first_bias, second, second_bias):
    rows = KY_BLOCK * NX
    slope = math.sqrt(2.0 / math.pi)

    def body(fh, fl, fb, sh, sl, sb, spec, high_ref, low_ref, deriv_ref, gate_ref):
        sides = [split(side) for side in both_sides(spec)]
        results = []
        for b in range(NB):
            left = tuple(window((sides[0][k], sides[1][k]), b) for k in range(2))
            v = dot3(left, (fh[block_span(b), :], fl[block_span(b), :]))
            v = v + fb[:, slim_span(b)]
            square = v * v
            t = jnp.tanh(slope * (v + 0.044715 * (v * square)))
            upper = 0.5 * (1.0 + t)
            outer = split(v * upper)
            high_ref[:, slim_span(b)] = outer[0]
            low_ref[:, slim_span(b)] = outer[1]
            deriv_ref[:, slim_span(b)] = upper + (0.5 * slope) * v * (1.0 - t * t) * (
                1.0 + (3 * 0.044715) * square
            )
            results.append(dot3(outer, (sh[:, block_span(b)], sl[:, block_span(b)])))
        for r, side in enumerate(spread(results)):
            t = jnp.tanh((side + sb[r : r + 1, :]) * (1.0 / shrink_level))
            gate_ref[:, r] = (t * t).reshape(KY_BLOCK, NX, C)

    slim = pl.BlockSpec((rows, NB * SLIM), lambda i: (i, 0))
    total = NX * NY
    return pl.pallas_call(
        body,
        grid=(NY // KY_BLOCK,),
        in_specs=[
            whole_block(WIDE, SLIM),
            whole_block(WIDE, SLIM),
            whole_block(1, NB * SLIM),
            whole_block(SLIM, WIDE),
            whole_block(SLIM, WIDE),
            whole_block(2, C),
            plane_block(),
        ],
        out_specs=[slim, slim, slim, plane_block()],
        out_shape=[
            jax.ShapeDtypeStruct((total, NB * SLIM), bf16),
            jax.ShapeDtypeStruct((total, NB * SLIM), bf16),
            jax.ShapeDtypeStruct((total, NB * SLIM), f32),
            jax.ShapeDtypeStruct((NY, 2, NX, C), f32),
        ],
        compiler_params=pltpu.CompilerParams(vmem_limit_bytes=VMEM),
        cost_estimate=mix_cost(2, 5),
        name="mix_front",
    )(*first, first_bias, *second, second_bias, spectrum)


def mix_back(gradient, spectrum, kept, first_back, second_back):
    rows = KY_BLOCK * NX
    along = (((0,), (0,)), ((), ()))

    def body(
        fh, fl, sh, sl, grad, spec, high_ref, low_ref, deriv_ref, gate_ref,
        out, one_ref, two_ref, bias_one_ref, bias_two_ref,
    ):
        @pl.when(pl.program_id(0) == 0)
        def _():
            for ref in (one_ref, two_ref, bias_one_ref, bias_two_ref):
                ref[...] = jnp.zeros_like(ref)

        grads = [g * t for g, t in zip(both_sides(grad), both_sides(gate_ref))]
        for r in range(2):
            bias_two_ref[r] += jnp.sum(grads[r].reshape(rows // 8, 8, C), axis=0)
        grads = [split(g) for g in grads]
        sides = [split(side) for side in both_sides(spec)]
        results = []
        for b in range(NB):
            two = tuple(window((grads[0][k], grads[1][k]), b) for k in range(2))
            outer = (high_ref[:, slim_span(b)], low_ref[:, slim_span(b)])
            two_ref[:, block_span(b)] += dot3(outer, two, along)
            one = dot3(two, (sh[block_span(b), :], sl[block_span(b), :]))
            one = one * deriv_ref[:, slim_span(b)]
            bias_one_ref[:, slim_span(b)] += jnp.sum(one.reshape(rows // 8, 8, SLIM), axis=0)
            one = split(one)
            left = tuple(window((sides[0][k], sides[1][k]), b) for k in range(2))
            one_ref[block_span(b), :] += dot3(left, one, along)
            results.append(dot3(one, (fh[:, block_span(b)], fl[:, block_span(b)])))
        for r, side in enumerate(spread(results)):
            out[:, r] = side.reshape(KY_BLOCK, NX, C)

    slim = pl.BlockSpec((rows, NB * SLIM), lambda i: (i, 0))
    return pl.pallas_call(
        body,
        grid=(NY // KY_BLOCK,),
        in_specs=[
            whole_block(SLIM, WIDE),
            whole_block(SLIM, WIDE),
            whole_block(WIDE, SLIM),
            whole_block(WIDE, SLIM),
            plane_block(),
            plane_block(),
            slim,
            slim,
            slim,
            plane_block(),
        ],
        out_specs=[
            plane_block(),
            whole_block(WIDE, SLIM),
            whole_block(SLIM, WIDE),
            whole_block(8, NB * SLIM),
            whole_block(2, 8, C),
        ],
        out_shape=[
            jax.ShapeDtypeStruct((NY, 2, NX, C), f32),
            jax.ShapeDtypeStruct((WIDE, SLIM), f32),
            jax.ShapeDtypeStruct((SLIM, WIDE), f32),
            jax.ShapeDtypeStruct((8, NB * SLIM), f32),
            jax.ShapeDtypeStruct((2, 8, C), f32),
        ],
        compiler_params=pltpu.CompilerParams(vmem_limit_bytes=VMEM),
        cost_estimate=mix_cost(4, 7),
        name="mix_back",
    )(*first_back, *second_back, gradient, spectrum, *kept)


def shards_planes(state_field, cotangent, first_weight, first_bias, second_weight, second_bias):
    nx, ny = lax.axis_size("px"), lax.axis_size("py")
    me_x, me_y = lax.axis_index("px"), lax.axis_index("py")
    places = [(dx, dy) for dx in range(nx) for dy in range(ny)]
    chunks = KZ // (nx * ny)
    xl, yl = NX // nx, NY // ny
    cells = xl * yl

    owner = jnp.stack([(me_x + dx) % nx * ny + (me_y + dy) % ny for dx, dy in places])
    kz = (owner[:, None] * chunks + jnp.arange(chunks, dtype=jnp.int32)).reshape(-1)
    cosine, sine = angle_tables(NZ, kz, jnp.arange(NZ, dtype=jnp.int32))
    depth = jnp.stack([cosine, -sine], axis=1)
    eye = jnp.eye(8, dtype=f32)
    depth = jnp.einsum("krz,ij->krijz", depth, eye, precision=highest)
    doubling = jnp.where(kz == 0, 1.0, 2.0).astype(f32)[:, None, None, None, None]
    size = 8 * NZ
    depth_table = depth.reshape(size, size)
    depth_doubled = (depth * doubling).reshape(size, size)

    x_at = ((me_x - jnp.arange(nx)) % nx)[:, None] * xl + jnp.arange(xl)
    y_at = ((me_y - jnp.arange(ny)) % ny)[:, None] * yl + jnp.arange(yl)
    cosine, sine = angle_tables(NY, jnp.arange(NY), y_at.reshape(-1))
    cols_table = jnp.concatenate(
        [jnp.concatenate([cosine, sine], axis=1), jnp.concatenate([-sine, cosine], axis=1)], axis=0
    )
    cosine, sine = angle_tables(NX, jnp.arange(NX), x_at.reshape(-1))
    rows_table = jnp.concatenate(
        [
            jnp.stack([cosine, sine], axis=2).reshape(NX, 2 * NX),
            jnp.stack([-sine, cosine], axis=2).reshape(NX, 2 * NX),
        ],
        axis=0,
    )

    def moved(value, place, way):
        dx, dy = place
        if dx == 0 and dy == 0:
            return value
        pairs = [
            (a * ny + b, (a + way * dx) % nx * ny + (b + way * dy) % ny)
            for a in range(nx)
            for b in range(ny)
        ]
        return lax.ppermute(value, ("px", "py"), pairs)

    def spectra(field, table):
        parts = depth_forward(field.reshape(cells * NZ, C), table, len(places) * chunks, cells)
        arrived = [
            [moved(parts[at * chunks + j], place, 1) for at, place in enumerate(places)]
            for j in range(chunks)
        ]
        return [plane_forward(arrived[j], cols_table, rows_table, nx, ny) for j in range(chunks)]

    full_first = pair_table(first_weight)
    full_second = pair_table(second_weight)
    first = stack_windows(full_first, 0)
    second = stack_windows(full_second, 1)
    slim_bias = jnp.pad(first_bias, ((0, 0), (0, 0), (0, LANES - BS)))
    slim_bias = jnp.transpose(slim_bias, (1, 0, 2)).reshape(1, NB * SLIM)
    wide_bias = second_bias.reshape(2, C)

    spectrum = spectra(state_field, depth_table)
    kept = [mix_front(s, halves(first), slim_bias, halves(second), wide_bias) for s in spectrum]
    gradient = spectra(cotangent, depth_doubled)
    backs = [
        mix_back(g, s, k, halves(first.T), halves(second.T))
        for g, s, k in zip(gradient, spectrum, kept)
    ]
    total_freq = state_field.shape[0] * lax.axis_size("dp") * NX * NY * KZ
    norm_factor = 1.0 / math.sqrt(total_freq)
    table_one, table_two, bias_one, bias_two = [
        sum(back[i] for back in backs) * norm_factor for i in range(1, 5)
    ]
    bias_one = jnp.sum(bias_one, axis=0).reshape(NB, 2, LANES)[:, :, :BS]
    sums = lax.psum(
        (
            fold_pairs(unstack_windows(table_one, 0)),
            jnp.transpose(bias_one, (1, 0, 2)),
            fold_pairs(unstack_windows(table_two, 1)),
            jnp.sum(bias_two, axis=1).reshape(2, NB, BS),
        ),
        ("dp", "px", "py"),
    )
    returned = [None] * (len(places) * chunks)
    for j in range(chunks):
        parts = plane_back(backs[j][0], cols_table.T, rows_table.T, nx, ny)
        for at, place in enumerate(places):
            returned[at * chunks + j] = moved(parts[at], place, -1)
    state_grad = depth_back(
        returned, cotangent.reshape(cells * NZ, C), depth_table.T, cells
    ).reshape(cotangent.shape)
    return (state_grad, sums[0], sums[1], sums[2], sums[3])


def solution(mesh):
    in_specs = (
        P("dp", "px", "py", None, None),
        P("dp", "px", "py", None, None),
        P(),
        P(),
        P(),
        P(),
    )
    out_specs = (P("dp", "px", "py", None, None), P(), P(), P(), P())
    planes = KZ % (mesh.shape["px"] * mesh.shape["py"]) == 0
    shards = shards_planes if planes else shards_plain
    return jax.shard_map(shards, mesh=mesh, in_specs=in_specs, out_specs=out_specs, check_vma=False)
```

```python
import math

import jax
import jax.numpy as jnp
from jax import lax
from jax.experimental import pallas as pl
from jax.experimental.pallas import tpu as pltpu
from jax.sharding import PartitionSpec as P

NX = 64
NY = 64
NZ = 32
NB = 4
BS = 96
KZ = 16


shrink_level = 0.25
highest = lax.Precision.HIGHEST


def complex_table(length, modes):
    row_ids = jnp.arange(length, dtype=jnp.int32)[:, None]
    col_ids = jnp.arange(modes, dtype=jnp.int32)[None, :]
    angles = (row_ids * col_ids % length).astype(jnp.float32) * (2.0 * math.pi / length)
    factor = 1.0 / math.sqrt(length)
    cosine = jnp.cos(angles) * factor
    sine_part = jnp.sin(angles) * factor
    upper_half = jnp.stack([cosine, -sine_part], axis=1)
    lower_half = jnp.stack([sine_part, cosine], axis=1)
    return jnp.stack([upper_half, lower_half], axis=0)


def pair_table(weight):
    real_part = weight[0]
    imag_part = weight[1]
    upper_half = jnp.stack([real_part, imag_part], axis=2)
    lower_half = jnp.stack([-imag_part, real_part], axis=2)
    return jnp.stack([upper_half, lower_half], axis=0)


def fold_pairs(pair_grads):
    return jnp.stack(
        [
            pair_grads[0, :, :, 0] + pair_grads[1, :, :, 1],
            pair_grads[0, :, :, 1] - pair_grads[1, :, :, 0],
        ]
    )


def contract(pattern, left_side, right_side):
    return jnp.einsum(
        pattern, left_side, right_side, precision=highest, preferred_element_type=jnp.float32
    )


def along_rows(spectral, rows_table):
    return contract("rmsxyzc,rxqk->qmskyzc", spectral, rows_table)


def along_cols(spectral, cols_table):
    return contract("rmsxyzc,ryqk->qmsxkzc", spectral, cols_table)


def back_rows(spectral, rows_table):
    return contract("qmskyzc,rxqk->rmsxyzc", spectral, rows_table)


def back_cols(spectral, cols_table):
    return contract("qmsxkzc,ryqk->rmsxyzc", spectral, cols_table)


def back_depth(spectral, depth_table):
    return contract("qmsxykc,zqk->msxyzc", spectral, depth_table)


def to_spectrum(fields, depth_table, rows_table, cols_table):
    spectral = contract("msxyzc,zqk->qmsxykc", fields, depth_table)
    spectral = along_cols(
        lax.all_to_all(spectral, "py", split_axis=5, concat_axis=4, tiled=True),
        cols_table=cols_table,
    )
    spectral = along_rows(
        lax.all_to_all(spectral, "px", split_axis=4, concat_axis=3, tiled=True),
        rows_table=rows_table,
    )
    return spectral


def to_field(spectral, depth_table, rows_table, cols_table):
    spectral = back_rows(spectral, rows_table)
    spectral = back_cols(
        lax.all_to_all(spectral, "px", split_axis=3, concat_axis=4, tiled=True),
        cols_table=cols_table,
    )
    result = back_depth(
        lax.all_to_all(spectral, "py", split_axis=4, concat_axis=5, tiled=True),
        depth_table=depth_table,
    )
    return result


def mix_forward(flat_in, first_table, first_bias, second_table, second_bias):
    pre_one = contract("rfbi,rbiqo->qfbo", flat_in, first_table) + first_bias[:, None]
    outer_one, gelu_back = jax.vjp(jax.nn.gelu, pre_one)
    pre_two = contract("rfbi,rbiqo->qfbo", outer_one, second_table) + second_bias[:, None]
    return (outer_one, gelu_back, pre_two)


def shards_plain(state_field, cotangent, first_weight, first_bias, second_weight, second_bias):
    depth_table = complex_table(NZ, KZ)[0]
    rows_table = complex_table(NX, NX)
    cols_table = complex_table(NY, NY)
    full_first = pair_table(first_weight)
    full_second = pair_table(second_weight)
    group_count = NB
    kz_block = lax.axis_index("py")
    kz_local = KZ // lax.axis_size("py")
    kz_global = kz_block * kz_local + jnp.arange(kz_local, dtype=jnp.int32)
    spectral_in = to_spectrum(state_field[None], depth_table, rows_table, cols_table)
    flat_in = spectral_in.reshape(2, -1, group_count, BS)
    outer_one, gelu_back, pre_two = mix_forward(
        flat_in, full_first, first_bias, full_second, second_bias
    )
    raw_gradient = to_spectrum(cotangent[None], depth_table, rows_table, cols_table)
    shape_full = spectral_in.shape
    doubling = jnp.where(kz_global == 0, 1.0, 2.0).astype(jnp.float32)[:, None]
    gradient_in = (raw_gradient * doubling).reshape(2, -1, group_count, BS)
    grad_two = gradient_in * jnp.tanh(pre_two / shrink_level) ** 2
    table_two = contract("rfbi,qfbo->rbiqo", outer_one, grad_two)
    grad_outer = contract("qfbo,rbiqo->rfbi", grad_two, full_second)
    grad_one = gelu_back(grad_outer)[0]
    table_one = contract("rfbi,qfbo->rbiqo", flat_in, grad_one)
    grad_spec = contract("qfbo,rbiqo->rfbi", grad_one, full_first)
    bias_one = jnp.sum(grad_one, axis=1)
    bias_two = jnp.sum(grad_two, axis=1)
    total_freq = state_field.shape[0] * lax.axis_size("dp") * NX * NY * KZ
    norm_factor = 1.0 / math.sqrt(total_freq)
    sums = lax.psum(
        (
            fold_pairs(table_one) * norm_factor,
            bias_one * norm_factor,
            fold_pairs(table_two) * norm_factor,
            bias_two * norm_factor,
        ),
        ("dp", "px", "py"),
    )
    spatial = to_field(grad_spec.reshape(shape_full), depth_table, rows_table, cols_table)[0]
    state_grad = (cotangent.astype(jnp.float32) + spatial).astype(jnp.bfloat16)
    return (state_grad, sums[0], sums[1], sums[2], sums[3])


C = NB * BS
LANES = 128
GROUPS = C // LANES
CELL_BLOCK = 64
KY_BLOCK = 8
VMEM = 60 * 1024 * 1024
f32 = jnp.float32
bf16 = jnp.bfloat16


def first_group(block):
    return block * BS // LANES


def group_count_of(block):
    return ((block + 1) * BS - 1) // LANES - first_group(block) + 1


WINDOWS = [(first_group(b), group_count_of(b)) for b in range(NB)]


def halves(values):
    high = lax.reduce_precision(values, 8, 7)
    return high.astype(bf16), (values - high).astype(bf16)


def split(values):
    high = values.astype(bf16)
    return high, (values - high.astype(f32)).astype(bf16)


def dot(left, right, dims=(((1,), (0,)), ((), ()))):
    return lax.dot_general(left, right, dims, preferred_element_type=f32)


def dot3(left, right, dims=(((1,), (0,)), ((), ()))):
    return (
        dot(left[0], right[0], dims) + dot(left[1], right[0], dims) + dot(left[0], right[1], dims)
    )


def table_dot(wide, low, values):
    high, rest = split(values)
    return dot(wide, jnp.concatenate([high, rest], axis=0)) + dot(low, high)


def angle_tables(length, rows, cols):
    angles = (rows[:, None] * cols[None, :] % length).astype(f32) * (2.0 * math.pi / length)
    factor = 1.0 / math.sqrt(length)
    return jnp.cos(angles) * factor, jnp.sin(angles) * factor


def table_pair(table):
    high, low = halves(table)
    return jnp.concatenate([high, high], axis=1), low


def depth_forward(field, table, slots, cells):
    def body(high_ref, low_ref, field_ref, *outs):
        for step in range(CELL_BLOCK // 8):
            part = field_ref[pl.ds(step * 8 * NZ, 8 * NZ), :]
            result = dot(high_ref[...], part) + dot(low_ref[...], part)
            for place, out in enumerate(outs):
                for r in range(2):
                    row = (place * 2 + r) * 8
                    out[r, pl.ds(step * 8, 8), :] = result[row : row + 8]

    size = 8 * NZ
    whole = pl.BlockSpec((size, size), lambda i: (0, 0))
    return pl.pallas_call(
        body,
        grid=(cells // CELL_BLOCK,),
        in_specs=[whole, whole, pl.BlockSpec((CELL_BLOCK * NZ, C), lambda i: (i, 0))],
        out_specs=[pl.BlockSpec((2, CELL_BLOCK, C), lambda i: (0, i, 0))] * slots,
        out_shape=[jax.ShapeDtypeStruct((2, cells, C), f32)] * slots,
        compiler_params=pltpu.CompilerParams(vmem_limit_bytes=VMEM),
        cost_estimate=pl.CostEstimate(
            flops=cells * 32 * C * size * 4, bytes_accessed=cells * 32 * C * 6, transcendentals=0
        ),
        name="depth_forward",
    )(*halves(table), field)


def depth_back(parts, cotangent, table, cells):
    slots = len(parts)

    def body(wide_ref, low_ref, cot_ref, *refs):
        out = refs[-1]
        for step in range(CELL_BLOCK // 8):
            rows = pl.ds(step * 8, 8)
            stacked = jnp.concatenate(
                [refs[place][r, rows, :] for place in range(slots) for r in range(2)], axis=0
            )
            here = pl.ds(step * 8 * NZ, 8 * NZ)
            spatial = table_dot(wide_ref[...], low_ref[...], stacked)
            out[here, :] = (cot_ref[here, :].astype(f32) + spatial).astype(bf16)

    size = 8 * NZ
    block = pl.BlockSpec((CELL_BLOCK * NZ, C), lambda i: (i, 0))
    return pl.pallas_call(
        body,
        grid=(cells // CELL_BLOCK,),
        in_specs=[
            pl.BlockSpec((size, 2 * size), lambda i: (0, 0)),
            pl.BlockSpec((size, size), lambda i: (0, 0)),
            block,
        ]
        + [pl.BlockSpec((2, CELL_BLOCK, C), lambda i: (0, i, 0))] * slots,
        out_specs=block,
        out_shape=jax.ShapeDtypeStruct((cells * NZ, C), bf16),
        compiler_params=pltpu.CompilerParams(vmem_limit_bytes=VMEM),
        cost_estimate=pl.CostEstimate(
            flops=cells * 32 * C * size * 6, bytes_accessed=cells * 32 * C * 8, transcendentals=0
        ),
        name="depth_back",
    )(*table_pair(table), cotangent, *parts)


def plane_call(body, operands, in_shapes, out_shapes, rows, name):
    vmem = pl.BlockSpec(memory_space=pltpu.VMEM)
    return pl.pallas_call(
        body,
        in_specs=[vmem] * len(operands),
        out_specs=[vmem] * len(out_shapes),
        out_shape=out_shapes,
        scratch_shapes=[pltpu.VMEM((GROUPS, rows, LANES), f32)],
        compiler_params=pltpu.CompilerParams(vmem_limit_bytes=VMEM),
        cost_estimate=pl.CostEstimate(
            flops=2 * 2 * NX * NY * C * 256 * 2 * 3,
            bytes_accessed=2 * NX * NY * C * 8,
            transcendentals=0,
        ),
        name=name,
    )(*operands)


def lanes_of(group):
    return slice(group * LANES, (group + 1) * LANES)


def plane_forward(parts, cols_table, rows_table, nx, ny):
    xl, yl = NX // nx, NY // ny
    pitch = NY + 8

    def body(cw, cl, rw, rl, *refs):
        ins, out, mid = refs[: nx * ny], refs[nx * ny], refs[nx * ny + 1]
        for dx in range(nx):

            def columns(i, carry, dx=dx):
                here = pl.ds(pl.multiple_of(i * yl, yl), yl)
                stacked = jnp.concatenate(
                    [ins[dx * ny + dy][r, here, :] for r in range(2) for dy in range(ny)], axis=0
                )
                result = table_dot(cw[...], cl[...], stacked)
                for r in range(2):
                    start = pl.multiple_of(((dx * xl + i) * 2 + r) * pitch, 8)
                    for g in range(GROUPS):
                        mid[g, pl.ds(start, NY), :] = result[r * NY : (r + 1) * NY, lanes_of(g)]
                return carry

            lax.fori_loop(0, xl, columns, 0, unroll=4)

        def across(ky, carry):
            stacked = jnp.concatenate(
                [mid[g, pl.ds(ky, 2 * NX, stride=pitch), :] for g in range(GROUPS)], axis=1
            )
            out[ky] = table_dot(rw[...], rl[...], stacked).reshape(2, NX, C)
            return carry

        lax.fori_loop(0, NY, across, 0, unroll=4)

    return plane_call(
        body,
        (*table_pair(cols_table), *table_pair(rows_table), *parts),
        None,
        [jax.ShapeDtypeStruct((NY, 2, NX, C), f32)],
        2 * NX * pitch,
        "plane_forward",
    )[0]


def plane_back(spectrum, cols_table, rows_table, nx, ny):
    xl, yl = NX // nx, NY // ny
    pitch = 2 * NX + 8

    def body(cw, cl, rw, rl, spec, *refs):
        outs, mid = refs[: nx * ny], refs[nx * ny]

        def across(ky, carry):
            result = table_dot(rw[...], rl[...], spec[ky].reshape(2 * NX, C))
            start = pl.multiple_of(ky * pitch, 8)
            for g in range(GROUPS):
                mid[g, pl.ds(start, 2 * NX), :] = result[:, lanes_of(g)]
            return carry

        lax.fori_loop(0, NY, across, 0, unroll=4)
        for dx in range(nx):

            def columns(i, carry, dx=dx):
                stacked = jnp.concatenate(
                    [
                        jnp.concatenate(
                            [
                                mid[g, pl.ds((dx * xl + i) * 2 + r, NY, stride=pitch), :]
                                for g in range(GROUPS)
                            ],
                            axis=1,
                        )
                        for r in range(2)
                    ],
                    axis=0,
                )
                result = table_dot(cw[...], cl[...], stacked)
                here = pl.ds(pl.multiple_of(i * yl, yl), yl)
                for r in range(2):
                    for dy in range(ny):
                        row = (r * ny + dy) * yl
                        outs[dx * ny + dy][r, here, :] = result[row : row + yl]
                return carry

            lax.fori_loop(0, xl, columns, 0, unroll=4)

    return plane_call(
        body,
        (*table_pair(cols_table), *table_pair(rows_table), spectrum),
        None,
        [jax.ShapeDtypeStruct((2, xl * yl, C), f32)] * (nx * ny),
        NY * pitch,
        "plane_back",
    )


def window(pair, block):
    start, count = WINDOWS[block]
    lanes = slice(start * LANES, (start + count) * LANES)
    return jnp.concatenate([pair[0][:, lanes], pair[1][:, lanes]], axis=1)


def spread(results):
    sides = []
    for r in range(2):
        groups = [None] * GROUPS
        for block, result in enumerate(results):
            start, count = WINDOWS[block]
            for g in range(count):
                at = r * count + g
                part = result[:, at * LANES : (at + 1) * LANES]
                groups[start + g] = part if groups[start + g] is None else groups[start + g] + part
        sides.append(jnp.concatenate(groups, axis=1))
    return sides


def offset_of(block):
    return block * BS - WINDOWS[block][0] * LANES


def stack_windows(table, axes):
    pieces = []
    for block in range(NB):
        count = WINDOWS[block][1]
        before = offset_of(block)
        wide = (before, count * LANES - before - BS)
        slim = (0, LANES - BS)
        sides = (wide, slim) if axes == 0 else (slim, wide)
        piece = jnp.pad(table[:, block], ((0, 0), sides[0], (0, 0), sides[1]))
        piece = piece.reshape(2 * piece.shape[1], -1)
        pieces.append(piece)
    return jnp.concatenate(pieces, axis=axes)


def unstack_windows(stacked, axes):
    pieces = []
    at = 0
    for block in range(NB):
        count = WINDOWS[block][1]
        size = 2 * count * LANES
        before = offset_of(block)
        if axes == 0:
            piece = stacked[at : at + size].reshape(2, count * LANES, 2, LANES)
            piece = piece[:, before : before + BS, :, :BS]
        else:
            piece = stacked[:, at : at + size].reshape(2, LANES, 2, count * LANES)
            piece = piece[:, :BS, :, before : before + BS]
        pieces.append(piece)
        at += size
    return jnp.stack(pieces, axis=1)


OFFSETS = [sum(2 * w[1] * LANES for w in WINDOWS[:b]) for b in range(NB + 1)]
WIDE = OFFSETS[NB]
SLIM = 2 * LANES


def block_span(block):
    return slice(OFFSETS[block], OFFSETS[block + 1])


def slim_span(block):
    return slice(block * SLIM, (block + 1) * SLIM)


def plane_block():
    return pl.BlockSpec((KY_BLOCK, 2, NX, C), lambda i: (i, 0, 0, 0))


def whole_block(*shape):
    return pl.BlockSpec(shape, lambda i: (0,) * len(shape))


def mix_cost(count, reads):
    rows = NX * NY
    return pl.CostEstimate(
        flops=rows * WIDE * SLIM * 2 * 3 * count,
        bytes_accessed=rows * 2 * C * 4 * reads,
        transcendentals=rows * 2 * C * 2,
    )


def both_sides(ref):
    rows = KY_BLOCK * NX
    return ref[:, 0].reshape(rows, C), ref[:, 1].reshape(rows, C)


def mix_front(spectrum, first, first_bias, second, second_bias):
    rows = KY_BLOCK * NX
    slope = math.sqrt(2.0 / math.pi)

    def body(fh, fl, fb, sh, sl, sb, spec, high_ref, low_ref, deriv_ref, gate_ref):
        sides = [split(side) for side in both_sides(spec)]
        results = []
        for b in range(NB):
            left = tuple(window((sides[0][k], sides[1][k]), b) for k in range(2))
            v = dot3(left, (fh[block_span(b), :], fl[block_span(b), :]))
            v = v + fb[:, slim_span(b)]
            square = v * v
            t = jnp.tanh(slope * (v + 0.044715 * (v * square)))
            upper = 0.5 * (1.0 + t)
            outer = split(v * upper)
            high_ref[:, slim_span(b)] = outer[0]
            low_ref[:, slim_span(b)] = outer[1]
            deriv_ref[:, slim_span(b)] = upper + (0.5 * slope) * v * (1.0 - t * t) * (
                1.0 + (3 * 0.044715) * square
            )
            results.append(dot3(outer, (sh[:, block_span(b)], sl[:, block_span(b)])))
        for r, side in enumerate(spread(results)):
            t = jnp.tanh((side + sb[r : r + 1, :]) * (1.0 / shrink_level))
            gate_ref[:, r] = (t * t).reshape(KY_BLOCK, NX, C)

    slim = pl.BlockSpec((rows, NB * SLIM), lambda i: (i, 0))
    total = NX * NY
    return pl.pallas_call(
        body,
        grid=(NY // KY_BLOCK,),
        in_specs=[
            whole_block(WIDE, SLIM),
            whole_block(WIDE, SLIM),
            whole_block(1, NB * SLIM),
            whole_block(SLIM, WIDE),
            whole_block(SLIM, WIDE),
            whole_block(2, C),
            plane_block(),
        ],
        out_specs=[slim, slim, slim, plane_block()],
        out_shape=[
            jax.ShapeDtypeStruct((total, NB * SLIM), bf16),
            jax.ShapeDtypeStruct((total, NB * SLIM), bf16),
            jax.ShapeDtypeStruct((total, NB * SLIM), f32),
            jax.ShapeDtypeStruct((NY, 2, NX, C), f32),
        ],
        compiler_params=pltpu.CompilerParams(vmem_limit_bytes=VMEM),
        cost_estimate=mix_cost(2, 5),
        name="mix_front",
    )(*first, first_bias, *second, second_bias, spectrum)


def mix_back(gradient, spectrum, kept, first_back, second_back):
    rows = KY_BLOCK * NX
    along = (((0,), (0,)), ((), ()))

    def body(
        fh, fl, sh, sl, grad, spec, high_ref, low_ref, deriv_ref, gate_ref,
        out, one_ref, two_ref, bias_one_ref, bias_two_ref,
    ):
        @pl.when(pl.program_id(0) == 0)
        def _():
            for ref in (one_ref, two_ref, bias_one_ref, bias_two_ref):
                ref[...] = jnp.zeros_like(ref)

        grads = [g * t for g, t in zip(both_sides(grad), both_sides(gate_ref))]
        for r in range(2):
            bias_two_ref[r] += jnp.sum(grads[r].reshape(rows // 8, 8, C), axis=0)
        grads = [split(g) for g in grads]
        sides = [split(side) for side in both_sides(spec)]
        results = []
        for b in range(NB):
            two = tuple(window((grads[0][k], grads[1][k]), b) for k in range(2))
            outer = (high_ref[:, slim_span(b)], low_ref[:, slim_span(b)])
            two_ref[:, block_span(b)] += dot3(outer, two, along)
            one = dot3(two, (sh[block_span(b), :], sl[block_span(b), :]))
            one = one * deriv_ref[:, slim_span(b)]
            bias_one_ref[:, slim_span(b)] += jnp.sum(one.reshape(rows // 8, 8, SLIM), axis=0)
            one = split(one)
            left = tuple(window((sides[0][k], sides[1][k]), b) for k in range(2))
            one_ref[block_span(b), :] += dot3(left, one, along)
            results.append(dot3(one, (fh[:, block_span(b)], fl[:, block_span(b)])))
        for r, side in enumerate(spread(results)):
            out[:, r] = side.reshape(KY_BLOCK, NX, C)

    slim = pl.BlockSpec((rows, NB * SLIM), lambda i: (i, 0))
    return pl.pallas_call(
        body,
        grid=(NY // KY_BLOCK,),
        in_specs=[
            whole_block(SLIM, WIDE),
            whole_block(SLIM, WIDE),
            whole_block(WIDE, SLIM),
            whole_block(WIDE, SLIM),
            plane_block(),
            plane_block(),
            slim,
            slim,
            slim,
            plane_block(),
        ],
        out_specs=[
            plane_block(),
            whole_block(WIDE, SLIM),
            whole_block(SLIM, WIDE),
            whole_block(8, NB * SLIM),
            whole_block(2, 8, C),
        ],
        out_shape=[
            jax.ShapeDtypeStruct((NY, 2, NX, C), f32),
            jax.ShapeDtypeStruct((WIDE, SLIM), f32),
            jax.ShapeDtypeStruct((SLIM, WIDE), f32),
            jax.ShapeDtypeStruct((8, NB * SLIM), f32),
            jax.ShapeDtypeStruct((2, 8, C), f32),
        ],
        compiler_params=pltpu.CompilerParams(vmem_limit_bytes=VMEM),
        cost_estimate=mix_cost(4, 7),
        name="mix_back",
    )(*first_back, *second_back, gradient, spectrum, *kept)


def shards_planes(state_field, cotangent, first_weight, first_bias, second_weight, second_bias):
    nx, ny = lax.axis_size("px"), lax.axis_size("py")
    me_x, me_y = lax.axis_index("px"), lax.axis_index("py")
    places = [(dx, dy) for dx in range(nx) for dy in range(ny)]
    chunks = KZ // (nx * ny)
    xl, yl = NX // nx, NY // ny
    cells = xl * yl

    owner = jnp.stack([(me_x + dx) % nx * ny + (me_y + dy) % ny for dx, dy in places])
    kz = (owner[:, None] * chunks + jnp.arange(chunks, dtype=jnp.int32)).reshape(-1)
    cosine, sine = angle_tables(NZ, kz, jnp.arange(NZ, dtype=jnp.int32))
    depth = jnp.stack([cosine, -sine], axis=1)
    eye = jnp.eye(8, dtype=f32)
    depth = jnp.einsum("krz,ij->krijz", depth, eye, precision=highest)
    doubling = jnp.where(kz == 0, 1.0, 2.0).astype(f32)[:, None, None, None, None]
    size = 8 * NZ
    depth_table = depth.reshape(size, size)
    depth_doubled = (depth * doubling).reshape(size, size)

    x_at = ((me_x - jnp.arange(nx)) % nx)[:, None] * xl + jnp.arange(xl)
    y_at = ((me_y - jnp.arange(ny)) % ny)[:, None] * yl + jnp.arange(yl)
    cosine, sine = angle_tables(NY, jnp.arange(NY), y_at.reshape(-1))
    cols_table = jnp.concatenate(
        [jnp.concatenate([cosine, sine], axis=1), jnp.concatenate([-sine, cosine], axis=1)], axis=0
    )
    cosine, sine = angle_tables(NX, jnp.arange(NX), x_at.reshape(-1))
    rows_table = jnp.concatenate(
        [
            jnp.stack([cosine, sine], axis=2).reshape(NX, 2 * NX),
            jnp.stack([-sine, cosine], axis=2).reshape(NX, 2 * NX),
        ],
        axis=0,
    )

    def moved(value, place, way):
        dx, dy = place
        if dx == 0 and dy == 0:
            return value
        pairs = [
            (a * ny + b, (a + way * dx) % nx * ny + (b + way * dy) % ny)
            for a in range(nx)
            for b in range(ny)
        ]
        return lax.ppermute(value, ("px", "py"), pairs)

    def spectra(field, table):
        parts = depth_forward(field.reshape(cells * NZ, C), table, len(places) * chunks, cells)
        arrived = [
            [moved(parts[at * chunks + j], place, 1) for at, place in enumerate(places)]
            for j in range(chunks)
        ]
        return [plane_forward(arrived[j], cols_table, rows_table, nx, ny) for j in range(chunks)]

    full_first = pair_table(first_weight)
    full_second = pair_table(second_weight)
    first = stack_windows(full_first, 0)
    second = stack_windows(full_second, 1)
    slim_bias = jnp.pad(first_bias, ((0, 0), (0, 0), (0, LANES - BS)))
    slim_bias = jnp.transpose(slim_bias, (1, 0, 2)).reshape(1, NB * SLIM)
    wide_bias = second_bias.reshape(2, C)

    spectrum = spectra(state_field, depth_table)
    kept = [mix_front(s, halves(first), slim_bias, halves(second), wide_bias) for s in spectrum]
    gradient = spectra(cotangent, depth_doubled)
    backs = [
        mix_back(g, s, k, halves(first.T), halves(second.T))
        for g, s, k in zip(gradient, spectrum, kept)
    ]
    total_freq = state_field.shape[0] * lax.axis_size("dp") * NX * NY * KZ
    norm_factor = 1.0 / math.sqrt(total_freq)
    table_one, table_two, bias_one, bias_two = [
        sum(back[i] for back in backs) * norm_factor for i in range(1, 5)
    ]
    bias_one = jnp.sum(bias_one, axis=0).reshape(NB, 2, LANES)[:, :, :BS]
    shares = (
        fold_pairs(unstack_windows(table_one, 0)),
        jnp.transpose(bias_one, (1, 0, 2)),
        fold_pairs(unstack_windows(table_two, 1)),
        jnp.sum(bias_two, axis=1).reshape(2, NB, BS),
    )
    packed = jnp.concatenate([share.reshape(-1) for share in shares]).reshape(-1, LANES)
    packed, last_back = lax.optimization_barrier((packed, backs[-1][0]))
    packed = lax.psum(packed, ("dp", "px", "py"))
    returned = [None] * (len(places) * chunks)
    for j in range(chunks):
        spectral = last_back if j == chunks - 1 else backs[j][0]
        parts = plane_back(spectral, cols_table.T, rows_table.T, nx, ny)
        for at, place in enumerate(places):
            part = parts[at]
            if j == chunks - 1 and at == len(places) - 1:
                part, packed = lax.optimization_barrier((part, packed))
            returned[at * chunks + j] = moved(part, place, -1)
    packed = packed.reshape(-1)
    sums = []
    for share in shares:
        sums.append(packed[: share.size].reshape(share.shape))
        packed = packed[share.size :]
    state_grad = depth_back(
        returned, cotangent.reshape(cells * NZ, C), depth_table.T, cells
    ).reshape(cotangent.shape)
    return (state_grad, sums[0], sums[1], sums[2], sums[3])


def solution(mesh):
    in_specs = (
        P("dp", "px", "py", None, None),
        P("dp", "px", "py", None, None),
        P(),
        P(),
        P(),
        P(),
    )
    out_specs = (P("dp", "px", "py", None, None), P(), P(), P(), P())
    planes = KZ % (mesh.shape["px"] * mesh.shape["py"]) == 0
    shards = shards_planes if planes else shards_plain
    return jax.shard_map(shards, mesh=mesh, in_specs=in_specs, out_specs=out_specs, check_vma=False)
```
